32 devices in a mesh: groups: 2 (over y), blk: 16 (over z, x, core).
Axes of the slice: x: 2, y: 2, z: 4, core: 2. Of those that a mesh axis runs over, the one named last changes fastest.
Arguments:
- txt_q: bfloat16 [1024, 1536], P(('groups', 'blk')), parts along dimension 0, may hold values from -40 to 40
- txt_k: bfloat16 [1024, 1536], P(('groups', 'blk')), parts along dimension 0, may hold values from -40 to 40
- txt_v: bfloat16 [1024, 1536], P(('groups', 'blk')), parts along dimension 0, may hold values from -6 to 6
- img_q: bfloat16 [2048, 1536], P(('groups', 'blk')), parts along dimension 0, may hold values from -6 to 6
- img_k: bfloat16 [2048, 1536], P(('groups', 'blk')), parts along dimension 0, may hold values from -6 to 6
- img_v: bfloat16 [2048, 1536], P(('groups', 'blk')), parts along dimension 0, may hold values from -6 to 6
- q_gain: float32 [128], replicated, may hold values from 0.35 to 3.5
- k_gain: float32 [128], replicated, may hold values from 0.35 to 3.5
- places: int32 [2048], P(('groups', 'blk')), parts along dimension 0, may hold values from 0 to 1023, each once
Outputs:
- txt_out: bfloat16 [1024, 1536], P(('groups', 'blk')), parts along dimension 0
- img_out: bfloat16 [2048, 1536], P(('groups', 'blk')), parts along dimension 0
The draws below stay inside these ranges and needn't reach their ends.
There are 2 independent parts, one for each index of `groups`. The reference program is written for one: setup_inputs(seed, part) draws one part's arguments, and reference() takes and returns one part's arrays. A program takes and returns all parts, laid end to end along the dimension named above; an argument that names none is the same for every part. Nothing has to cross between parts.
All inputs are finite; a program needn't handle non-finite values.
Results may differ from the reference program's by a relative error of at most 0.0055.
The reference program's roundings to bfloat16 on the way count: a program that leaves them out, or rounds other values in their place, can miss the bound.
Values may be sent and summed in bfloat16 or wider, within the bound.
A program may use at most 64 MiB of HBM per device.

```python
import math
import jax
import jax.numpy as jnp
from jax import lax

HEADS = 12
HEAD_DIM = 128
TEXT = 512
GRID_W = 256
WIDTH = 1536
IMG = 1024


def text_pair(key):
    keys_drawn = jax.random.normal(jax.random.fold_in(key, 101), (TEXT, WIDTH), jnp.float32)
    queries_drawn = jax.random.normal(jax.random.fold_in(key, 102), (TEXT, WIDTH), jnp.float32)
    return (jnp.clip(queries_drawn, -40.0, 40.0), jnp.clip(keys_drawn, -40.0, 40.0))


def draw_txt_q(key, part):
    return text_pair(key)[0].astype(jnp.bfloat16)


def draw_txt_k(key, part):
    return text_pair(key)[1].astype(jnp.bfloat16)


def block_levels(stream_key, dims, shards, low, high):
    level, own = 1.0, jax.random.fold_in(stream_key, 6)
    for position, parts in shards:
        draws = jnp.exp(jax.random.uniform(jax.random.fold_in(own, position), (parts,), jnp.float32, low / len(shards), high / len(shards)))
        level = level * jnp.repeat(draws, dims[position] // parts).reshape([-1 if axis == position else 1 for axis in range(len(dims))])
    return level


def noise(key, extent, deviation, most, pieces=(), kind=jnp.bfloat16):
    loudness = block_levels(key, extent, pieces, -0.22, 0.18) if pieces else 1.0
    values = jax.random.normal(key, extent, jnp.float32) * deviation * loudness
    return jnp.minimum(jnp.maximum(values, -most), most).astype(kind)


def setup_inputs(seed: int = 0, part: int = 0) -> dict:
    key_list = jax.random.split(jax.random.key(seed), 10)
    part_keys = jax.random.split(jax.random.fold_in(key_list[9], part), 10)
    return {
        "txt_q": draw_txt_q(jax.random.fold_in(jax.random.fold_in(key_list[9], part), 71), part),
        "txt_k": draw_txt_k(jax.random.fold_in(jax.random.fold_in(key_list[9], part), 71), part),
        "txt_v": noise(part_keys[2], (TEXT, WIDTH), 1.0, 6.0, ((0, 16),)),
        "img_q": noise(part_keys[3], (IMG, WIDTH), 1.0, 6.0, ((0, 16),)),
        "img_k": noise(part_keys[4], (IMG, WIDTH), 1.0, 6.0, ((0, 16),)),
        "img_v": noise(part_keys[5], (IMG, WIDTH), 1.0, 6.0, ((0, 16),)),
        "q_gain": jnp.clip(jnp.exp(jax.random.uniform(key_list[6], (HEAD_DIM,), jnp.float32, math.log(0.35), math.log(3.5))), 0.35, 3.5),
        "k_gain": jnp.clip(jnp.exp(jax.random.uniform(key_list[7], (HEAD_DIM,), jnp.float32, math.log(0.35), math.log(3.5))), 0.35, 3.5),
        "places": jax.random.permutation(part_keys[8], IMG).astype(jnp.int32),
    }


rope_theta = 10000.0

def normed(values, gain):
    row_count = values.shape[0]
    heads = values.astype(jnp.float32).reshape(row_count, HEADS, HEAD_DIM)
    mean_sq = lax.optimization_barrier(jnp.mean(heads * heads, axis=-1, keepdims=True))
    return heads * lax.rsqrt(mean_sq + 1e-06) * gain

def rotate(heads, places):
    row_count = heads.shape[0]
    row_pos = (places // GRID_W).astype(jnp.float32)[:, None]
    col_pos = (places % GRID_W).astype(jnp.float32)[:, None]
    index = jnp.arange(64, dtype=jnp.float32)[None, :]
    freq_row = jnp.exp(-(index - 8.0) / 28.0 * jnp.log(rope_theta))
    freq_col = jnp.exp(-(index - 36.0) / 28.0 * jnp.log(rope_theta))
    angle = jnp.where(index < 8.0, 0.0 * row_pos, jnp.where(index < 36.0, row_pos * freq_row, col_pos * freq_col))
    cosine = jnp.cos(angle)[:, None, :]
    sine = jnp.sin(angle)[:, None, :]
    pairs = heads.reshape(row_count, HEADS, 64, 2)
    first = pairs[..., 0]
    second = pairs[..., 1]
    turned = jnp.stack([first * cosine - second * sine, first * sine + second * cosine], axis=-1)
    return turned.reshape(row_count, HEADS, HEAD_DIM)

def one_head(operands):
    queries, keys, values = operands
    row_count = queries.shape[0]
    block_size = 256 if row_count % 256 == 0 else row_count
    blocked = queries.reshape(row_count // block_size, block_size, HEAD_DIM)

    def one_block(query_block):
        scores = jnp.dot(query_block, keys.T, preferred_element_type=jnp.float32) / jnp.sqrt(jnp.float32(HEAD_DIM))
        top = lax.optimization_barrier(jnp.max(scores, axis=-1, keepdims=True))
        expo = jnp.exp(scores - top)
        total = lax.optimization_barrier(jnp.sum(expo, axis=-1, keepdims=True))
        mixed = jnp.dot(expo.astype(jnp.bfloat16), values, preferred_element_type=jnp.float32)
        return (mixed / total).astype(jnp.bfloat16)
    return lax.map(one_block, blocked).reshape(row_count, HEAD_DIM)

def reference(txt_q, txt_k, txt_v, img_q, img_k, img_v, q_gain, k_gain, places):
    queries = jnp.concatenate([normed(txt_q, q_gain).astype(jnp.bfloat16), rotate(normed(img_q, q_gain), places).astype(jnp.bfloat16)], axis=0)
    keys = jnp.concatenate([normed(txt_k, k_gain).astype(jnp.bfloat16), rotate(normed(img_k, k_gain), places).astype(jnp.bfloat16)], axis=0)
    values = jnp.concatenate([txt_v, img_v], axis=0)
    row_count = values.shape[0]
    values = values.reshape(row_count, HEADS, HEAD_DIM)
    result = lax.map(one_head, (jnp.transpose(queries, (1, 0, 2)), jnp.transpose(keys, (1, 0, 2)), jnp.transpose(values, (1, 0, 2))))
    result = jnp.transpose(result, (1, 0, 2)).reshape(row_count, HEADS * HEAD_DIM)
    return (result[:TEXT], result[TEXT:])
```

```python
import functools
import math

import jax
import jax.numpy as jnp
from jax import lax
from jax.experimental import pallas as pl
from jax.experimental.pallas import tpu as pltpu
from jax.sharding import PartitionSpec as P

HEADS = 12
HEAD_DIM = 128
GRID_W = 256


rope_theta = 10000.0


def from_partner(block, axis, apart):
    count = lax.axis_size(axis)
    route = []
    for low in range(count):
        high = low | 1 << apart
        if high != low and high < count:
            route += [(low, high), (high, low)]
    return lax.ppermute(block, axis, route)


def passed_along(block, axis, distance):
    devices = range(lax.axis_size(axis))
    route = [((i - distance) % len(devices), i) for i in devices]
    return lax.ppermute(block, axis, route)


def normed(values, gain):
    row_count = values.shape[0]
    heads = values.astype(jnp.float32).reshape(row_count, HEADS, HEAD_DIM)
    mean_sq = jnp.mean(heads * heads, axis=-1, keepdims=True)
    return heads * lax.rsqrt(mean_sq + 1e-06) * gain


def rotate(heads, places):
    row_count = heads.shape[0]
    row_pos = (places // GRID_W).astype(jnp.float32)[:, None]
    col_pos = (places % GRID_W).astype(jnp.float32)[:, None]
    index = jnp.arange(64, dtype=jnp.float32)[None, :]
    freq_row = jnp.exp(-(index - 8.0) / 28.0 * jnp.log(rope_theta))
    freq_col = jnp.exp(-(index - 36.0) / 28.0 * jnp.log(rope_theta))
    angle = jnp.where(
        index < 8.0, 0.0 * row_pos, jnp.where(index < 36.0, row_pos * freq_row, col_pos * freq_col)
    )
    cosine = jnp.cos(angle)[:, None, :]
    sine = jnp.sin(angle)[:, None, :]
    pairs = heads.reshape(row_count, HEADS, 64, 2)
    first = pairs[..., 0]
    second = pairs[..., 1]
    turned = jnp.stack([first * cosine - second * sine, first * sine + second * cosine], axis=-1)
    return turned.reshape(row_count, HEADS, HEAD_DIM)


def update(state_tuple, queries, pair_block):
    running_max, running_sum, running_acc = state_tuple
    key_block = pair_block[0]
    value_block = pair_block[1]
    scores = jnp.einsum("rhd,nhd->rhn", queries, key_block, preferred_element_type=jnp.float32)
    scores = scores / jnp.sqrt(jnp.float32(HEAD_DIM))
    new_max = jnp.maximum(running_max, jnp.max(scores, axis=-1))
    fade_out = jnp.exp(running_max - new_max)
    expo = jnp.exp(scores - new_max[..., None])
    new_sum = running_sum * fade_out + jnp.sum(expo, axis=-1)
    added = jnp.einsum(
        "rhn,nhd->rhd", expo.astype(jnp.bfloat16), value_block, preferred_element_type=jnp.float32
    )
    new_acc = running_acc * fade_out[..., None] + added
    return (new_max, new_sum, new_acc)


def regroup_swap(piece, bit_number):
    return from_partner(piece, "blk", bit_number)


def restore_swap(piece, bit_number):
    return from_partner(piece, "blk", bit_number)


def among_four(stacked, mover):
    index_here = lax.axis_index("blk")
    for bit_number in (0, 1):
        position = 1 - bit_number
        own_bit = index_here >> bit_number & 1
        kept_half = lax.dynamic_index_in_dim(stacked, own_bit, position, keepdims=False)
        sent_half = lax.dynamic_index_in_dim(stacked, 1 - own_bit, position, keepdims=False)
        received = mover(sent_half, bit_number)
        stacked = jnp.where(
            own_bit == 0,
            jnp.stack([kept_half, received], axis=position),
            jnp.stack([received, kept_half], axis=position),
        )
    return stacked


def move_upward(pair_block):
    return passed_along(pair_block, "blk", 4)


def move_downward(pair_block):
    return passed_along(pair_block, "blk", -4)


def per_device(txt_q, txt_k, txt_v, img_q, img_k, img_v, q_gain, k_gain, places):
    txt_count = txt_q.shape[0]
    img_count = img_q.shape[0]
    local_count = txt_count + img_count
    quarter = HEADS // 4
    queries = jnp.concatenate(
        [
            normed(txt_q, q_gain).astype(jnp.bfloat16),
            rotate(normed(img_q, q_gain), places).astype(jnp.bfloat16),
        ],
        axis=0,
    )
    keys_local = jnp.concatenate(
        [
            normed(txt_k, k_gain).astype(jnp.bfloat16),
            rotate(normed(img_k, k_gain), places).astype(jnp.bfloat16),
        ],
        axis=0,
    )
    values_local = jnp.concatenate([txt_v, img_v], axis=0).reshape(local_count, HEADS, HEAD_DIM)
    stacked = jnp.stack([queries, keys_local, values_local], axis=1).reshape(
        local_count, 3, 4, quarter, HEAD_DIM
    )
    stacked = jnp.transpose(stacked, (2, 0, 1, 3, 4)).reshape(
        2, 2, local_count, 3, quarter, HEAD_DIM
    )
    grouped = among_four(stacked, regroup_swap).reshape(4 * local_count, 3, quarter, HEAD_DIM)
    group_q = grouped[:, 0]
    own_pair = jnp.stack([grouped[:, 1], grouped[:, 2]], axis=0)
    group_rows = 4 * local_count
    blocks = lax.axis_size("blk") // 4
    soft_state = (
        jnp.full((group_rows, quarter), -jnp.inf, jnp.float32),
        jnp.zeros((group_rows, quarter), jnp.float32),
        jnp.zeros((group_rows, quarter, HEAD_DIM), jnp.float32),
    )
    soft_state = update(soft_state, group_q, own_pair)
    downward_turns = (blocks - 1) // 2

    def both_turn(turn, loop_state):
        upward, downward, inner = loop_state
        upward = move_upward(upward)
        downward = move_downward(downward)
        inner = update(inner, group_q, upward)
        inner = update(inner, group_q, downward)
        return (upward, downward, inner)

    upward, downward, soft_state = lax.fori_loop(
        0, downward_turns, both_turn, (own_pair, own_pair, soft_state)
    )
    upward = move_upward(upward)
    soft_state = update(soft_state, group_q, upward)
    running_max, running_sum, running_acc = soft_state
    result = (running_acc / running_sum[..., None]).astype(jnp.bfloat16)
    result = result.reshape(2, 2, local_count, quarter, HEAD_DIM)
    returned = among_four(result, restore_swap).reshape(4, local_count, quarter, HEAD_DIM)
    returned = jnp.transpose(returned, (1, 0, 2, 3)).reshape(local_count, HEADS * HEAD_DIM)
    return (returned[:txt_count], returned[txt_count:])


MESH = pl.DeviceIdType.MESH
COLUMN = 4


def angles(places):
    row_pos = (places // GRID_W).astype(jnp.float32)[:, None]
    col_pos = (places % GRID_W).astype(jnp.float32)[:, None]
    lane = lax.broadcasted_iota(jnp.int32, (1, HEAD_DIM), 1)
    index = (lane // 2).astype(jnp.float32)
    freq_row = jnp.exp(-(index - 8.0) / 28.0 * jnp.log(rope_theta))
    freq_col = jnp.exp(-(index - 36.0) / 28.0 * jnp.log(rope_theta))
    angle = jnp.where(
        index < 8.0, 0.0 * row_pos, jnp.where(index < 36.0, row_pos * freq_row, col_pos * freq_col)
    )
    sine = jnp.sin(angle)
    return jnp.cos(angle), jnp.where(lane % 2 == 0, -sine, sine)


def attention_kernel(
    layers, own_heads,
    txt_q, txt_k, txt_v, img_q, img_k, img_v, q_gain, k_gain, cosine, sine,
    txt_out, img_out,
    stage, own, from_x, from_core, out_stage, out_all,
    z_send, z_recv, x_send, x_recv, c_send, c_recv, o_send, o_recv,
):
    texts = txt_q.shape[0]
    tokens = texts + img_q.shape[0]
    rows = layers * tokens
    me = lax.axis_index("blk")
    layer = me // COLUMN
    spot = me % COLUMN
    x_peer = layer * COLUMN + (spot + 2) % COLUMN
    core_peer = layer * COLUMN + (spot // 2) * 2 + (spot + 1) % 2

    def at_layer(apart):
        return (layer + apart) % layers

    barrier = pltpu.get_barrier_semaphore()
    peers = [at_layer(apart) * COLUMN + spot for apart in range(1, layers)] + [x_peer, core_peer]
    for peer in peers:
        pl.semaphore_signal(barrier, inc=1, device_id={"blk": peer}, device_id_type=MESH)

    even = lax.broadcasted_iota(jnp.int32, (1, HEAD_DIM), 1) % 2 == 0

    def norm(ref, columns, gain):
        x = ref[:, columns].astype(jnp.float32)
        mean_sq = jnp.mean(x * x, axis=-1, keepdims=True)
        return x * lax.rsqrt(mean_sq + 1e-06) * gain[...]

    def turn(y):
        other = jnp.where(even, pltpu.roll(y, HEAD_DIM - 1, 1), pltpu.roll(y, 1, 1))
        return (y * cosine[...] + other * sine[...]).astype(jnp.bfloat16)

    def prepare(head, to, *where):
        columns = pl.ds(pl.multiple_of(head * HEAD_DIM, HEAD_DIM), HEAD_DIM)

        def put(kind, first, second):
            to[(where[0], kind, where[1], pl.ds(0, texts))] = first
            to[(where[0], kind, where[1], pl.ds(texts, tokens - texts))] = second

        put(0, norm(txt_q, columns, q_gain).astype(jnp.bfloat16), turn(norm(img_q, columns, q_gain)))
        put(1, norm(txt_k, columns, k_gain).astype(jnp.bfloat16), turn(norm(img_k, columns, k_gain)))
        put(2, txt_v[:, columns], img_v[:, columns])

    order = [layers // 2] + [a for a in range(1, layers) if a != layers // 2]

    def z_copy(i, apart):
        to = at_layer(apart)
        return pltpu.make_async_remote_copy(
            src_ref=stage.at[i, :, apart], dst_ref=own.at[i, :, layer],
            send_sem=z_send.at[i, apart], recv_sem=z_recv.at[i, layer],
            device_id={"blk": to * COLUMN + spot}, device_id_type=MESH,
        )

    def z_arrival(i, apart):
        source = at_layer(layers - apart)
        return pltpu.make_async_remote_copy(
            src_ref=stage.at[i, :, apart], dst_ref=own.at[i, :, source],
            send_sem=z_send.at[i, apart], recv_sem=z_recv.at[i, source],
            device_id={"blk": at_layer(apart) * COLUMN + spot}, device_id_type=MESH,
        )

    def x_copy(i, source):
        return pltpu.make_async_remote_copy(
            src_ref=own.at[i, pl.ds(1, 2), source], dst_ref=from_x.at[i, :, source],
            send_sem=x_send.at[i, source], recv_sem=x_recv.at[i, source],
            device_id={"blk": x_peer}, device_id_type=MESH,
        )

    def core_copy(i, which):
        src = own.at[i, pl.ds(1, 2)] if which == 0 else from_x.at[i]
        return pltpu.make_async_remote_copy(
            src_ref=src, dst_ref=from_core.at[i, which],
            send_sem=c_send.at[i, which], recv_sem=c_recv.at[i, which],
            device_id={"blk": core_peer}, device_id_type=MESH,
        )

    def out_copy(i, apart):
        to = at_layer(apart)
        head = layer * own_heads + i
        return pltpu.make_async_remote_copy(
            src_ref=out_stage.at[i, to], dst_ref=out_all.at[head],
            send_sem=o_send.at[i, apart], recv_sem=o_recv.at[head],
            device_id={"blk": to * COLUMN + spot}, device_id_type=MESH,
        )

    def out_arrival(i, apart):
        head = at_layer(apart) * own_heads + i
        return pltpu.make_async_remote_copy(
            src_ref=out_stage.at[i, layer], dst_ref=out_all.at[head],
            send_sem=o_send.at[i, apart], recv_sem=o_recv.at[head],
            device_id={"blk": at_layer(apart) * COLUMN + spot}, device_id_type=MESH,
        )

    prepare(at_layer(order[0]) * own_heads, stage, 0, order[0])
    pl.semaphore_wait(barrier, len(peers))
    z_copy(0, order[0]).start()
    for i in range(own_heads):
        for apart in order:
            if i or apart != order[0]:
                prepare(at_layer(apart) * own_heads + i, stage, i, apart)
                z_copy(i, apart).start()
        prepare(layer * own_heads + i, own, i, layer)
        x_copy(i, layer).start()

    factor = math.log2(math.e) / math.sqrt(HEAD_DIM)

    @pl.loop(0, own_heads)
    def _(i):
        for apart in order:
            z_arrival(i, apart).wait_recv()
            x_copy(i, at_layer(layers - apart)).start()
        core_copy(i, 0).start()
        queries = own[i, 0].reshape(rows, HEAD_DIM)

        def block(state, keys, values):
            scores = lax.dot_general(
                queries, keys.reshape(rows, HEAD_DIM), (((1,), (1,)), ((), ())),
                preferred_element_type=jnp.float32,
            ) * factor
            top = jnp.max(scores, axis=-1, keepdims=True)
            if state is not None:
                top = jnp.maximum(top, state[0])
            expo = jnp.exp2(scores - top)
            total = jnp.sum(expo, axis=-1, keepdims=True)
            mixed = jnp.dot(
                expo.astype(jnp.bfloat16), values.reshape(rows, HEAD_DIM),
                preferred_element_type=jnp.float32,
            )
            if state is not None:
                fade = jnp.exp2(state[0] - top)
                total = total + state[1] * fade
                mixed = mixed + state[2] * fade
            return top, total, mixed

        state = block(None, own[i, 1], own[i, 2])
        for source in range(layers):
            x_copy(i, source).wait_recv()
        core_copy(i, 1).start()
        state = block(state, from_x[i, 0], from_x[i, 1])
        core_copy(i, 0).wait_recv()
        state = block(state, from_core[i, 0, 0], from_core[i, 0, 1])
        core_copy(i, 1).wait_recv()
        _, total, mixed = block(state, from_core[i, 1, 0], from_core[i, 1, 1])
        out_stage[i] = (mixed / total).astype(jnp.bfloat16).reshape(layers, tokens, HEAD_DIM)
        for apart in order:
            out_copy(i, apart).start()
        out_all[layer * own_heads + i] = out_stage[i, layer]

    for i in range(own_heads):
        for apart in order:
            out_arrival(i, apart).wait_recv()
    for head in range(layers * own_heads):
        columns = slice(head * HEAD_DIM, (head + 1) * HEAD_DIM)
        txt_out[:, columns] = out_all[head, :texts]
        img_out[:, columns] = out_all[head, texts:]

    @pl.loop(0, own_heads)
    def _(i):
        for apart in order:
            z_copy(i, apart).wait_send()
            out_copy(i, apart).wait_send()
        for source in range(layers):
            x_copy(i, source).wait_send()
        core_copy(i, 0).wait_send()
        core_copy(i, 1).wait_send()


def per_device_fused(layers, txt_q, txt_k, txt_v, img_q, img_k, img_v, q_gain, k_gain, places):
    own_heads = HEADS // layers
    tokens = txt_q.shape[0] + img_q.shape[0]
    cosine, sine = angles(places)
    bf16, dma = jnp.bfloat16, pltpu.SemaphoreType.DMA
    block = (tokens, HEAD_DIM)
    return pl.pallas_call(
        functools.partial(attention_kernel, layers, own_heads),
        out_shape=(
            jax.ShapeDtypeStruct(txt_q.shape, bf16),
            jax.ShapeDtypeStruct(img_q.shape, bf16),
        ),
        in_specs=[pl.BlockSpec(memory_space=pltpu.VMEM)] * 10,
        out_specs=(pl.BlockSpec(memory_space=pltpu.VMEM),) * 2,
        scratch_shapes=[
            pltpu.VMEM((own_heads, 3, layers, *block), bf16),
            pltpu.VMEM((own_heads, 3, layers, *block), bf16),
            pltpu.VMEM((own_heads, 2, layers, *block), bf16),
            pltpu.VMEM((own_heads, 2, 2, layers, *block), bf16),
            pltpu.VMEM((own_heads, layers, *block), bf16),
            pltpu.VMEM((HEADS, *block), bf16),
            dma((own_heads, layers)), dma((own_heads, layers)),
            dma((own_heads, layers)), dma((own_heads, layers)),
            dma((own_heads, 2)), dma((own_heads, 2)),
            dma((own_heads, layers)), dma((HEADS,)),
        ],
        compiler_params=pltpu.CompilerParams(
            collective_id=0, has_side_effects=True, vmem_limit_bytes=40 * 1024 * 1024
        ),
    )(
        txt_q, txt_k, txt_v, img_q, img_k, img_v,
        q_gain.reshape(1, HEAD_DIM), k_gain.reshape(1, HEAD_DIM), cosine, sine,
    )


def per_device_any(txt_q, txt_k, txt_v, img_q, img_k, img_v, q_gain, k_gain, places):
    layers, left_over = divmod(lax.axis_size("blk"), COLUMN)
    whole_tiles = txt_q.shape[0] % 16 == 0 and img_q.shape[0] % 16 == 0
    fits = left_over == 0 and layers > 1 and HEADS % max(layers, 1) == 0 and whole_tiles
    part = functools.partial(per_device_fused, layers) if fits else per_device
    return part(txt_q, txt_k, txt_v, img_q, img_k, img_v, q_gain, k_gain, places)


def solution(mesh):
    placed = (
        P(("groups", "blk"), None),
        P(("groups", "blk"), None),
        P(("groups", "blk"), None),
        P(("groups", "blk"), None),
        P(("groups", "blk"), None),
        P(("groups", "blk"), None),
        P(),
        P(),
        P(("groups", "blk")),
    )
    return jax.shard_map(
        per_device_any,
        mesh=mesh,
        in_specs=placed,
        out_specs=(P(("groups", "blk"), None), P(("groups", "blk"), None)),
        check_vma=False,
    )
```

```python
import functools
import math

import jax
import jax.numpy as jnp
from jax import lax
from jax.experimental import pallas as pl
from jax.experimental.pallas import tpu as pltpu
from jax.sharding import PartitionSpec as P

HEADS = 12
HEAD_DIM = 128
GRID_W = 256


rope_theta = 10000.0


def from_partner(block, axis, apart):
    count = lax.axis_size(axis)
    route = []
    for low in range(count):
        high = low | 1 << apart
        if high != low and high < count:
            route += [(low, high), (high, low)]
    return lax.ppermute(block, axis, route)


def passed_along(block, axis, distance):
    devices = range(lax.axis_size(axis))
    route = [((i - distance) % len(devices), i) for i in devices]
    return lax.ppermute(block, axis, route)


def normed(values, gain):
    row_count = values.shape[0]
    heads = values.astype(jnp.float32).reshape(row_count, HEADS, HEAD_DIM)
    mean_sq = jnp.mean(heads * heads, axis=-1, keepdims=True)
    return heads * lax.rsqrt(mean_sq + 1e-06) * gain


def rotate(heads, places):
    row_count = heads.shape[0]
    row_pos = (places // GRID_W).astype(jnp.float32)[:, None]
    col_pos = (places % GRID_W).astype(jnp.float32)[:, None]
    index = jnp.arange(64, dtype=jnp.float32)[None, :]
    freq_row = jnp.exp(-(index - 8.0) / 28.0 * jnp.log(rope_theta))
    freq_col = jnp.exp(-(index - 36.0) / 28.0 * jnp.log(rope_theta))
    angle = jnp.where(
        index < 8.0, 0.0 * row_pos, jnp.where(index < 36.0, row_pos * freq_row, col_pos * freq_col)
    )
    cosine = jnp.cos(angle)[:, None, :]
    sine = jnp.sin(angle)[:, None, :]
    pairs = heads.reshape(row_count, HEADS, 64, 2)
    first = pairs[..., 0]
    second = pairs[..., 1]
    turned = jnp.stack([first * cosine - second * sine, first * sine + second * cosine], axis=-1)
    return turned.reshape(row_count, HEADS, HEAD_DIM)


def update(state_tuple, queries, pair_block):
    running_max, running_sum, running_acc = state_tuple
    key_block = pair_block[0]
    value_block = pair_block[1]
    scores = jnp.einsum("rhd,nhd->rhn", queries, key_block, preferred_element_type=jnp.float32)
    scores = scores / jnp.sqrt(jnp.float32(HEAD_DIM))
    new_max = jnp.maximum(running_max, jnp.max(scores, axis=-1))
    fade_out = jnp.exp(running_max - new_max)
    expo = jnp.exp(scores - new_max[..., None])
    new_sum = running_sum * fade_out + jnp.sum(expo, axis=-1)
    added = jnp.einsum(
        "rhn,nhd->rhd", expo.astype(jnp.bfloat16), value_block, preferred_element_type=jnp.float32
    )
    new_acc = running_acc * fade_out[..., None] + added
    return (new_max, new_sum, new_acc)


def regroup_swap(piece, bit_number):
    return from_partner(piece, "blk", bit_number)


def restore_swap(piece, bit_number):
    return from_partner(piece, "blk", bit_number)


def among_four(stacked, mover):
    index_here = lax.axis_index("blk")
    for bit_number in (0, 1):
        position = 1 - bit_number
        own_bit = index_here >> bit_number & 1
        kept_half = lax.dynamic_index_in_dim(stacked, own_bit, position, keepdims=False)
        sent_half = lax.dynamic_index_in_dim(stacked, 1 - own_bit, position, keepdims=False)
        received = mover(sent_half, bit_number)
        stacked = jnp.where(
            own_bit == 0,
            jnp.stack([kept_half, received], axis=position),
            jnp.stack([received, kept_half], axis=position),
        )
    return stacked


def move_upward(pair_block):
    return passed_along(pair_block, "blk", 4)


def move_downward(pair_block):
    return passed_along(pair_block, "blk", -4)


def per_device(txt_q, txt_k, txt_v, img_q, img_k, img_v, q_gain, k_gain, places):
    txt_count = txt_q.shape[0]
    img_count = img_q.shape[0]
    local_count = txt_count + img_count
    quarter = HEADS // 4
    queries = jnp.concatenate(
        [
            normed(txt_q, q_gain).astype(jnp.bfloat16),
            rotate(normed(img_q, q_gain), places).astype(jnp.bfloat16),
        ],
        axis=0,
    )
    keys_local = jnp.concatenate(
        [
            normed(txt_k, k_gain).astype(jnp.bfloat16),
            rotate(normed(img_k, k_gain), places).astype(jnp.bfloat16),
        ],
        axis=0,
    )
    values_local = jnp.concatenate([txt_v, img_v], axis=0).reshape(local_count, HEADS, HEAD_DIM)
    stacked = jnp.stack([queries, keys_local, values_local], axis=1).reshape(
        local_count, 3, 4, quarter, HEAD_DIM
    )
    stacked = jnp.transpose(stacked, (2, 0, 1, 3, 4)).reshape(
        2, 2, local_count, 3, quarter, HEAD_DIM
    )
    grouped = among_four(stacked, regroup_swap).reshape(4 * local_count, 3, quarter, HEAD_DIM)
    group_q = grouped[:, 0]
    own_pair = jnp.stack([grouped[:, 1], grouped[:, 2]], axis=0)
    group_rows = 4 * local_count
    blocks = lax.axis_size("blk") // 4
    soft_state = (
        jnp.full((group_rows, quarter), -jnp.inf, jnp.float32),
        jnp.zeros((group_rows, quarter), jnp.float32),
        jnp.zeros((group_rows, quarter, HEAD_DIM), jnp.float32),
    )
    soft_state = update(soft_state, group_q, own_pair)
    downward_turns = (blocks - 1) // 2

    def both_turn(turn, loop_state):
        upward, downward, inner = loop_state
        upward = move_upward(upward)
        downward = move_downward(downward)
        inner = update(inner, group_q, upward)
        inner = update(inner, group_q, downward)
        return (upward, downward, inner)

    upward, downward, soft_state = lax.fori_loop(
        0, downward_turns, both_turn, (own_pair, own_pair, soft_state)
    )
    upward = move_upward(upward)
    soft_state = update(soft_state, group_q, upward)
    running_max, running_sum, running_acc = soft_state
    result = (running_acc / running_sum[..., None]).astype(jnp.bfloat16)
    result = result.reshape(2, 2, local_count, quarter, HEAD_DIM)
    returned = among_four(result, restore_swap).reshape(4, local_count, quarter, HEAD_DIM)
    returned = jnp.transpose(returned, (1, 0, 2, 3)).reshape(local_count, HEADS * HEAD_DIM)
    return (returned[:txt_count], returned[txt_count:])


MESH = pl.DeviceIdType.MESH
COLUMN = 4


def angles(places):
    count = places.shape[1]
    square = (count, count)
    diagonal = lax.broadcasted_iota(jnp.int32, square, 0) == lax.broadcasted_iota(jnp.int32, square, 1)
    spread = jnp.broadcast_to(places.astype(jnp.float32), square)
    token = jnp.sum(jnp.where(diagonal, spread, 0.0), axis=1, keepdims=True).astype(jnp.int32)
    row_pos = (token // GRID_W).astype(jnp.float32)
    col_pos = (token % GRID_W).astype(jnp.float32)
    lane = lax.broadcasted_iota(jnp.int32, (1, HEAD_DIM), 1)
    index = (lane // 2).astype(jnp.float32)
    freq_row = jnp.exp(-(index - 8.0) / 28.0 * math.log(rope_theta))
    freq_col = jnp.exp(-(index - 36.0) / 28.0 * math.log(rope_theta))
    angle = jnp.where(
        index < 8.0, 0.0 * row_pos, jnp.where(index < 36.0, row_pos * freq_row, col_pos * freq_col)
    )
    sine = jnp.sin(angle)
    return jnp.cos(angle), jnp.where(lane % 2 == 0, -sine, sine)


def attention_kernel(
    layers, own_heads,
    txt_q_in, txt_k_in, txt_v_in, img_q_in, img_k_in, img_v_in, q_gain_in, k_gain_in, places_in,
    txt_out, img_out,
    txt_q, txt_k, txt_v, img_q, img_k, img_v, q_gain, k_gain, places,
    cosine, sine, load_sem,
    stage, own, from_x, from_core, out_stage, out_all,
    z_send, z_recv, q_send, q_recv, x_send, x_recv, c_send, c_recv, o_send, o_recv,
):
    texts = txt_q.shape[0]
    tokens = texts + img_q.shape[0]
    rows = layers * tokens
    me = lax.axis_index("blk")
    layer = me // COLUMN
    spot = me % COLUMN
    x_peer = layer * COLUMN + (spot + 2) % COLUMN
    core_peer = layer * COLUMN + (spot // 2) * 2 + (spot + 1) % 2

    loads = [
        pltpu.make_async_copy(source, to, load_sem.at[n])
        for n, (source, to) in enumerate((
            (places_in, places), (q_gain_in, q_gain), (k_gain_in, k_gain),
            (txt_q_in, txt_q), (img_q_in, img_q), (txt_k_in, txt_k),
            (img_k_in, img_k), (txt_v_in, txt_v), (img_v_in, img_v),
        ))
    ]
    for load in loads:
        load.start()

    def at_layer(apart):
        return (layer + apart) % layers

    barrier = pltpu.get_barrier_semaphore()
    peers = [at_layer(apart) * COLUMN + spot for apart in range(1, layers)] + [x_peer, core_peer]
    for peer in peers:
        pl.semaphore_signal(barrier, inc=1, device_id={"blk": peer}, device_id_type=MESH)

    even = lax.broadcasted_iota(jnp.int32, (1, HEAD_DIM), 1) % 2 == 0

    def norm(ref, columns, gain):
        x = ref[:, columns].astype(jnp.float32)
        mean_sq = jnp.mean(x * x, axis=-1, keepdims=True)
        return x * lax.rsqrt(mean_sq + 1e-06) * gain[...]

    def turn(y):
        other = jnp.where(even, pltpu.roll(y, HEAD_DIM - 1, 1), pltpu.roll(y, 1, 1))
        return (y * cosine[...] + other * sine[...]).astype(jnp.bfloat16)

    def columns_of(head):
        return pl.ds(pl.multiple_of(head * HEAD_DIM, HEAD_DIM), HEAD_DIM)

    def put(to, i, kind, slot, first, second):
        to[i, kind, slot, pl.ds(0, texts)] = first
        to[i, kind, slot, pl.ds(texts, tokens - texts)] = second

    def prepare_pair(head, to, i, slot):
        columns = columns_of(head)
        put(to, i, 1, slot, norm(txt_k, columns, k_gain).astype(jnp.bfloat16), turn(norm(img_k, columns, k_gain)))
        put(to, i, 2, slot, txt_v[:, columns], img_v[:, columns])

    def prepare_queries(head, to, i, slot):
        columns = columns_of(head)
        put(to, i, 0, slot, norm(txt_q, columns, q_gain).astype(jnp.bfloat16), turn(norm(img_q, columns, q_gain)))

    order = [layers // 2] + [a for a in range(1, layers) if a != layers // 2]
    PAIR, QUERY = (pl.ds(1, 2), z_send, z_recv), (pl.ds(0, 1), q_send, q_recv)

    def z_copy(what, i, apart):
        kinds, send, recv = what
        return pltpu.make_async_remote_copy(
            src_ref=stage.at[i, kinds, apart], dst_ref=own.at[i, kinds, layer],
            send_sem=send.at[i, apart], recv_sem=recv.at[i, layer],
            device_id={"blk": at_layer(apart) * COLUMN + spot}, device_id_type=MESH,
        )

    def z_arrival(what, i, apart):
        kinds, send, recv = what
        source = at_layer(layers - apart)
        return pltpu.make_async_remote_copy(
            src_ref=stage.at[i, kinds, apart], dst_ref=own.at[i, kinds, source],
            send_sem=send.at[i, apart], recv_sem=recv.at[i, source],
            device_id={"blk": at_layer(apart) * COLUMN + spot}, device_id_type=MESH,
        )

    def x_copy(i, source):
        return pltpu.make_async_remote_copy(
            src_ref=own.at[i, pl.ds(1, 2), source], dst_ref=from_x.at[i, :, source],
            send_sem=x_send.at[i, source], recv_sem=x_recv.at[i, source],
            device_id={"blk": x_peer}, device_id_type=MESH,
        )

    def core_copy(i, which):
        src = own.at[i, pl.ds(1, 2)] if which == 0 else from_x.at[i]
        return pltpu.make_async_remote_copy(
            src_ref=src, dst_ref=from_core.at[i, which],
            send_sem=c_send.at[i, which], recv_sem=c_recv.at[i, which],
            device_id={"blk": core_peer}, device_id_type=MESH,
        )

    def out_copy(i, apart):
        to = at_layer(apart)
        head = layer * own_heads + i
        return pltpu.make_async_remote_copy(
            src_ref=out_stage.at[i, to], dst_ref=out_all.at[head],
            send_sem=o_send.at[i, apart], recv_sem=o_recv.at[head],
            device_id={"blk": to * COLUMN + spot}, device_id_type=MESH,
        )

    def out_arrival(i, apart):
        head = at_layer(apart) * own_heads + i
        return pltpu.make_async_remote_copy(
            src_ref=out_stage.at[i, layer], dst_ref=out_all.at[head],
            send_sem=o_send.at[i, apart], recv_sem=o_recv.at[head],
            device_id={"blk": at_layer(apart) * COLUMN + spot}, device_id_type=MESH,
        )

    loads[0].wait()
    cosine[...], sine[...] = angles(places[...])
    for load in loads[1:]:
        load.wait()
    window = 2
    units = [(PAIR, i) for i in range(own_heads)] + [(QUERY, i) for i in range(own_heads)]

    def go_on(n, apart):
        z_copy(*units[n], apart).wait_send()
        if n + window < len(units):
            z_copy(*units[n + window], apart).start()

    for i in range(own_heads):
        for apart in order:
            prepare_pair(at_layer(apart) * own_heads + i, stage, i, apart)
            if i == 0 and apart == order[0]:
                pl.semaphore_wait(barrier, len(peers))
            if i < window:
                z_copy(PAIR, i, apart).start()
        prepare_pair(layer * own_heads + i, own, i, layer)
        x_copy(i, layer).start()
    for i in range(own_heads):
        for apart in order:
            prepare_queries(at_layer(apart) * own_heads + i, stage, i, apart)
        prepare_queries(layer * own_heads + i, own, i, layer)

    def relay(i):
        for source in range(layers):
            x_copy(i, source).wait_recv()
        core_copy(i, 1).start()

    for i in range(own_heads):
        for apart in order:
            z_arrival(PAIR, i, apart).wait_recv()
            x_copy(i, at_layer(layers - apart)).start()
            go_on(i, apart)
        core_copy(i, 0).start()
        if i:
            relay(i - 1)
    relay(own_heads - 1)

    factor = math.log2(math.e) / math.sqrt(HEAD_DIM)

    def step(i):
        for apart in order:
            z_arrival(QUERY, i, apart).wait_recv()
            go_on(own_heads + i, apart)
        queries = own[i, 0].reshape(rows, HEAD_DIM)

        def block(state, keys, values):
            scores = lax.dot_general(
                queries, keys.reshape(rows, HEAD_DIM), (((1,), (1,)), ((), ())),
                preferred_element_type=jnp.float32,
            ) * factor
            top = jnp.max(scores, axis=-1, keepdims=True)
            if state is not None:
                top = jnp.maximum(top, state[0])
            expo = jnp.exp2(scores - top)
            total = jnp.sum(expo, axis=-1, keepdims=True)
            mixed = jnp.dot(
                expo.astype(jnp.bfloat16), values.reshape(rows, HEAD_DIM),
                preferred_element_type=jnp.float32,
            )
            if state is not None:
                fade = jnp.exp2(state[0] - top)
                total = total + state[1] * fade
                mixed = mixed + state[2] * fade
            return top, total, mixed

        state = block(None, own[i, 1], own[i, 2])
        state = block(state, from_x[i, 0], from_x[i, 1])
        core_copy(i, 0).wait_recv()
        state = block(state, from_core[i, 0, 0], from_core[i, 0, 1])
        core_copy(i, 1).wait_recv()
        _, total, mixed = block(state, from_core[i, 1, 0], from_core[i, 1, 1])
        out_stage[i] = (mixed / total).astype(jnp.bfloat16).reshape(layers, tokens, HEAD_DIM)
        for apart in order:
            out_copy(i, apart).start()
        out_all[layer * own_heads + i] = out_stage[i, layer]

    for i in range(own_heads):
        step(i)

    for i in range(own_heads):
        for apart in order:
            out_arrival(i, apart).wait_recv()
    for head in range(layers * own_heads):
        columns = slice(head * HEAD_DIM, (head + 1) * HEAD_DIM)
        txt_out[:, columns] = out_all[head, :texts]
        img_out[:, columns] = out_all[head, texts:]

    for i in range(own_heads):
        for apart in order:
            out_copy(i, apart).wait_send()
        for source in range(layers):
            x_copy(i, source).wait_send()
        core_copy(i, 0).wait_send()
        core_copy(i, 1).wait_send()


def per_device_fused(layers, txt_q, txt_k, txt_v, img_q, img_k, img_v, q_gain, k_gain, places):
    own_heads = HEADS // layers
    tokens = txt_q.shape[0] + img_q.shape[0]
    bf16, dma = jnp.bfloat16, pltpu.SemaphoreType.DMA
    block = (tokens, HEAD_DIM)
    return pl.pallas_call(
        functools.partial(attention_kernel, layers, own_heads),
        out_shape=(
            jax.ShapeDtypeStruct(txt_q.shape, bf16),
            jax.ShapeDtypeStruct(img_q.shape, bf16),
        ),
        in_specs=[pl.BlockSpec(memory_space=pltpu.HBM)] * 9,
        out_specs=(pl.BlockSpec(memory_space=pltpu.VMEM),) * 2,
        scratch_shapes=[
            *[pltpu.VMEM(x.shape, bf16) for x in (txt_q, txt_k, txt_v, img_q, img_k, img_v)],
            pltpu.VMEM((1, HEAD_DIM), jnp.float32),
            pltpu.VMEM((1, HEAD_DIM), jnp.float32),
            pltpu.VMEM((1, places.shape[0]), jnp.int32),
            pltpu.VMEM((img_q.shape[0], HEAD_DIM), jnp.float32),
            pltpu.VMEM((img_q.shape[0], HEAD_DIM), jnp.float32),
            dma((9,)),
            pltpu.VMEM((own_heads, 3, layers, *block), bf16),
            pltpu.VMEM((own_heads, 3, layers, *block), bf16),
            pltpu.VMEM((own_heads, 2, layers, *block), bf16),
            pltpu.VMEM((own_heads, 2, 2, layers, *block), bf16),
            pltpu.VMEM((own_heads, layers, *block), bf16),
            pltpu.VMEM((HEADS, *block), bf16),
            dma((own_heads, layers)), dma((own_heads, layers)),
            dma((own_heads, layers)), dma((own_heads, layers)),
            dma((own_heads, layers)), dma((own_heads, layers)),
            dma((own_heads, 2)), dma((own_heads, 2)),
            dma((own_heads, layers)), dma((HEADS,)),
        ],
        compiler_params=pltpu.CompilerParams(
            collective_id=0, has_side_effects=True, vmem_limit_bytes=63 * 1024 * 1024
        ),
    )(
        txt_q, txt_k, txt_v, img_q, img_k, img_v,
        q_gain.reshape(1, HEAD_DIM), k_gain.reshape(1, HEAD_DIM),
        places.reshape(1, -1),
    )


def per_device_any(txt_q, txt_k, txt_v, img_q, img_k, img_v, q_gain, k_gain, places):
    layers, left_over = divmod(lax.axis_size("blk"), COLUMN)
    whole_tiles = txt_q.shape[0] % 16 == 0 and img_q.shape[0] % 16 == 0
    fits = left_over == 0 and layers > 1 and HEADS % max(layers, 1) == 0 and whole_tiles
    part = functools.partial(per_device_fused, layers) if fits else per_device
    return part(txt_q, txt_k, txt_v, img_q, img_k, img_v, q_gain, k_gain, places)


def solution(mesh):
    placed = (
        P(("groups", "blk"), None),
        P(("groups", "blk"), None),
        P(("groups", "blk"), None),
        P(("groups", "blk"), None),
        P(("groups", "blk"), None),
        P(("groups", "blk"), None),
        P(),
        P(),
        P(("groups", "blk")),
    )
    return jax.shard_map(
        per_device_any,
        mesh=mesh,
        in_specs=placed,
        out_specs=(P(("groups", "blk"), None), P(("groups", "blk"), None)),
        check_vma=False,
    )
```

```python
import functools
import math

import jax
import jax.numpy as jnp
from jax import lax
from jax.experimental import pallas as pl
from jax.experimental.pallas import tpu as pltpu
from jax.sharding import PartitionSpec as P

HEADS = 12
HEAD_DIM = 128
GRID_W = 256


rope_theta = 10000.0


def from_partner(block, axis, apart):
    count = lax.axis_size(axis)
    route = []
    for low in range(count):
        high = low | 1 << apart
        if high != low and high < count:
            route += [(low, high), (high, low)]
    return lax.ppermute(block, axis, route)


def passed_along(block, axis, distance):
    devices = range(lax.axis_size(axis))
    route = [((i - distance) % len(devices), i) for i in devices]
    return lax.ppermute(block, axis, route)


def normed(values, gain):
    row_count = values.shape[0]
    heads = values.astype(jnp.float32).reshape(row_count, HEADS, HEAD_DIM)
    mean_sq = jnp.mean(heads * heads, axis=-1, keepdims=True)
    return heads * lax.rsqrt(mean_sq + 1e-06) * gain


def rotate(heads, places):
    row_count = heads.shape[0]
    row_pos = (places // GRID_W).astype(jnp.float32)[:, None]
    col_pos = (places % GRID_W).astype(jnp.float32)[:, None]
    index = jnp.arange(64, dtype=jnp.float32)[None, :]
    freq_row = jnp.exp(-(index - 8.0) / 28.0 * jnp.log(rope_theta))
    freq_col = jnp.exp(-(index - 36.0) / 28.0 * jnp.log(rope_theta))
    angle = jnp.where(
        index < 8.0, 0.0 * row_pos, jnp.where(index < 36.0, row_pos * freq_row, col_pos * freq_col)
    )
    cosine = jnp.cos(angle)[:, None, :]
    sine = jnp.sin(angle)[:, None, :]
    pairs = heads.reshape(row_count, HEADS, 64, 2)
    first = pairs[..., 0]
    second = pairs[..., 1]
    turned = jnp.stack([first * cosine - second * sine, first * sine + second * cosine], axis=-1)
    return turned.reshape(row_count, HEADS, HEAD_DIM)


def update(state_tuple, queries, pair_block):
    running_max, running_sum, running_acc = state_tuple
    key_block = pair_block[0]
    value_block = pair_block[1]
    scores = jnp.einsum("rhd,nhd->rhn", queries, key_block, preferred_element_type=jnp.float32)
    scores = scores / jnp.sqrt(jnp.float32(HEAD_DIM))
    new_max = jnp.maximum(running_max, jnp.max(scores, axis=-1))
    fade_out = jnp.exp(running_max - new_max)
    expo = jnp.exp(scores - new_max[..., None])
    new_sum = running_sum * fade_out + jnp.sum(expo, axis=-1)
    added = jnp.einsum(
        "rhn,nhd->rhd", expo.astype(jnp.bfloat16), value_block, preferred_element_type=jnp.float32
    )
    new_acc = running_acc * fade_out[..., None] + added
    return (new_max, new_sum, new_acc)


def regroup_swap(piece, bit_number):
    return from_partner(piece, "blk", bit_number)


def restore_swap(piece, bit_number):
    return from_partner(piece, "blk", bit_number)


def among_four(stacked, mover):
    index_here = lax.axis_index("blk")
    for bit_number in (0, 1):
        position = 1 - bit_number
        own_bit = index_here >> bit_number & 1
        kept_half = lax.dynamic_index_in_dim(stacked, own_bit, position, keepdims=False)
        sent_half = lax.dynamic_index_in_dim(stacked, 1 - own_bit, position, keepdims=False)
        received = mover(sent_half, bit_number)
        stacked = jnp.where(
            own_bit == 0,
            jnp.stack([kept_half, received], axis=position),
            jnp.stack([received, kept_half], axis=position),
        )
    return stacked


def move_upward(pair_block):
    return passed_along(pair_block, "blk", 4)


def move_downward(pair_block):
    return passed_along(pair_block, "blk", -4)


def per_device(txt_q, txt_k, txt_v, img_q, img_k, img_v, q_gain, k_gain, places):
    txt_count = txt_q.shape[0]
    img_count = img_q.shape[0]
    local_count = txt_count + img_count
    quarter = HEADS // 4
    queries = jnp.concatenate(
        [
            normed(txt_q, q_gain).astype(jnp.bfloat16),
            rotate(normed(img_q, q_gain), places).astype(jnp.bfloat16),
        ],
        axis=0,
    )
    keys_local = jnp.concatenate(
        [
            normed(txt_k, k_gain).astype(jnp.bfloat16),
            rotate(normed(img_k, k_gain), places).astype(jnp.bfloat16),
        ],
        axis=0,
    )
    values_local = jnp.concatenate([txt_v, img_v], axis=0).reshape(local_count, HEADS, HEAD_DIM)
    stacked = jnp.stack([queries, keys_local, values_local], axis=1).reshape(
        local_count, 3, 4, quarter, HEAD_DIM
    )
    stacked = jnp.transpose(stacked, (2, 0, 1, 3, 4)).reshape(
        2, 2, local_count, 3, quarter, HEAD_DIM
    )
    grouped = among_four(stacked, regroup_swap).reshape(4 * local_count, 3, quarter, HEAD_DIM)
    group_q = grouped[:, 0]
    own_pair = jnp.stack([grouped[:, 1], grouped[:, 2]], axis=0)
    group_rows = 4 * local_count
    blocks = lax.axis_size("blk") // 4
    soft_state = (
        jnp.full((group_rows, quarter), -jnp.inf, jnp.float32),
        jnp.zeros((group_rows, quarter), jnp.float32),
        jnp.zeros((group_rows, quarter, HEAD_DIM), jnp.float32),
    )
    soft_state = update(soft_state, group_q, own_pair)
    downward_turns = (blocks - 1) // 2

    def both_turn(turn, loop_state):
        upward, downward, inner = loop_state
        upward = move_upward(upward)
        downward = move_downward(downward)
        inner = update(inner, group_q, upward)
        inner = update(inner, group_q, downward)
        return (upward, downward, inner)

    upward, downward, soft_state = lax.fori_loop(
        0, downward_turns, both_turn, (own_pair, own_pair, soft_state)
    )
    upward = move_upward(upward)
    soft_state = update(soft_state, group_q, upward)
    running_max, running_sum, running_acc = soft_state
    result = (running_acc / running_sum[..., None]).astype(jnp.bfloat16)
    result = result.reshape(2, 2, local_count, quarter, HEAD_DIM)
    returned = among_four(result, restore_swap).reshape(4, local_count, quarter, HEAD_DIM)
    returned = jnp.transpose(returned, (1, 0, 2, 3)).reshape(local_count, HEADS * HEAD_DIM)
    return (returned[:txt_count], returned[txt_count:])


MESH = pl.DeviceIdType.MESH
COLUMN = 4


def angles(places):
    count = places.shape[1]
    square = (count, count)
    diagonal = lax.broadcasted_iota(jnp.int32, square, 0) == lax.broadcasted_iota(jnp.int32, square, 1)
    spread = jnp.broadcast_to(places.astype(jnp.float32), square)
    token = jnp.sum(jnp.where(diagonal, spread, 0.0), axis=1, keepdims=True).astype(jnp.int32)
    row_pos = (token // GRID_W).astype(jnp.float32)
    col_pos = (token % GRID_W).astype(jnp.float32)
    lane = lax.broadcasted_iota(jnp.int32, (1, HEAD_DIM), 1)
    index = (lane // 2).astype(jnp.float32)
    freq_row = jnp.exp(-(index - 8.0) / 28.0 * math.log(rope_theta))
    freq_col = jnp.exp(-(index - 36.0) / 28.0 * math.log(rope_theta))
    angle = jnp.where(
        index < 8.0, 0.0 * row_pos, jnp.where(index < 36.0, row_pos * freq_row, col_pos * freq_col)
    )
    sine = jnp.sin(angle)
    return jnp.cos(angle), jnp.where(lane % 2 == 0, -sine, sine)


def attention_kernel(
    layers, own_heads,
    txt_q_in, txt_k_in, txt_v_in, img_q_in, img_k_in, img_v_in, q_gain_in, k_gain_in, places_in,
    txt_out, img_out,
    txt_q, txt_k, txt_v, img_q, img_k, img_v, q_gain, k_gain, places,
    cosine, sine, load_sem,
    stage, own, from_x, from_core, out_stage, out_all,
    z_send, z_recv, q_send, q_recv, x_send, x_recv, c_send, c_recv, o_send, o_recv,
):
    texts = txt_q.shape[0]
    tokens = texts + img_q.shape[0]
    rows = layers * tokens
    me = lax.axis_index("blk")
    layer = me // COLUMN
    spot = me % COLUMN
    x_peer = layer * COLUMN + (spot + 2) % COLUMN
    core_peer = layer * COLUMN + (spot // 2) * 2 + (spot + 1) % 2

    loads = [
        pltpu.make_async_copy(source, to, load_sem.at[n])
        for n, (source, to) in enumerate((
            (places_in, places), (q_gain_in, q_gain), (k_gain_in, k_gain),
            (txt_q_in, txt_q), (img_q_in, img_q), (txt_k_in, txt_k),
            (img_k_in, img_k), (txt_v_in, txt_v), (img_v_in, img_v),
        ))
    ]
    for load in loads:
        load.start()

    def at_layer(apart):
        return (layer + apart) % layers

    barrier = pltpu.get_barrier_semaphore()
    peers = [at_layer(apart) * COLUMN + spot for apart in range(1, layers)] + [x_peer, core_peer]
    for peer in peers:
        pl.semaphore_signal(barrier, inc=1, device_id={"blk": peer}, device_id_type=MESH)

    even = lax.broadcasted_iota(jnp.int32, (1, HEAD_DIM), 1) % 2 == 0

    def norm(ref, columns, gain):
        x = ref[:, columns].astype(jnp.float32)
        mean_sq = jnp.mean(x * x, axis=-1, keepdims=True)
        return x * lax.rsqrt(mean_sq + 1e-06) * gain[...]

    def turn(y):
        other = jnp.where(even, pltpu.roll(y, HEAD_DIM - 1, 1), pltpu.roll(y, 1, 1))
        return (y * cosine[...] + other * sine[...]).astype(jnp.bfloat16)

    def columns_of(head):
        return pl.ds(pl.multiple_of(head * HEAD_DIM, HEAD_DIM), HEAD_DIM)

    def put(to, i, kind, slot, first, second):
        to[i, kind, slot, pl.ds(0, texts)] = first
        to[i, kind, slot, pl.ds(texts, tokens - texts)] = second

    def prepare_pair(head, to, i, slot):
        columns = columns_of(head)
        put(to, i, 1, slot, norm(txt_k, columns, k_gain).astype(jnp.bfloat16), turn(norm(img_k, columns, k_gain)))
        put(to, i, 2, slot, txt_v[:, columns], img_v[:, columns])

    def prepare_queries(head, to, i, slot):
        columns = columns_of(head)
        put(to, i, 0, slot, norm(txt_q, columns, q_gain).astype(jnp.bfloat16), turn(norm(img_q, columns, q_gain)))

    order = list(range(1, layers))
    PAIR, QUERY = (pl.ds(1, 2), z_send, z_recv), (pl.ds(0, 1), q_send, q_recv)

    def z_copy(what, i, apart):
        kinds, send, recv = what
        return pltpu.make_async_remote_copy(
            src_ref=stage.at[i, kinds, apart], dst_ref=own.at[i, kinds, layer],
            send_sem=send.at[i, apart], recv_sem=recv.at[i, layer],
            device_id={"blk": at_layer(apart) * COLUMN + spot}, device_id_type=MESH,
        )

    def z_arrival(what, i, apart):
        kinds, send, recv = what
        source = at_layer(layers - apart)
        return pltpu.make_async_remote_copy(
            src_ref=stage.at[i, kinds, apart], dst_ref=own.at[i, kinds, source],
            send_sem=send.at[i, apart], recv_sem=recv.at[i, source],
            device_id={"blk": at_layer(apart) * COLUMN + spot}, device_id_type=MESH,
        )

    def x_copy(i, source):
        return pltpu.make_async_remote_copy(
            src_ref=own.at[i, pl.ds(1, 2), source], dst_ref=from_x.at[i, :, source],
            send_sem=x_send.at[i, source], recv_sem=x_recv.at[i, source],
            device_id={"blk": x_peer}, device_id_type=MESH,
        )

    def core_copy(i, which):
        src = own.at[i, pl.ds(1, 2)] if which == 0 else from_x.at[i]
        return pltpu.make_async_remote_copy(
            src_ref=src, dst_ref=from_core.at[i, which],
            send_sem=c_send.at[i, which], recv_sem=c_recv.at[i, which],
            device_id={"blk": core_peer}, device_id_type=MESH,
        )

    def out_copy(i, apart):
        to = at_layer(apart)
        head = layer * own_heads + i
        return pltpu.make_async_remote_copy(
            src_ref=out_stage.at[i, to], dst_ref=out_all.at[head],
            send_sem=o_send.at[i, apart], recv_sem=o_recv.at[head],
            device_id={"blk": to * COLUMN + spot}, device_id_type=MESH,
        )

    def out_arrival(i, apart):
        head = at_layer(apart) * own_heads + i
        return pltpu.make_async_remote_copy(
            src_ref=out_stage.at[i, layer], dst_ref=out_all.at[head],
            send_sem=o_send.at[i, apart], recv_sem=o_recv.at[head],
            device_id={"blk": at_layer(apart) * COLUMN + spot}, device_id_type=MESH,
        )

    loads[0].wait()
    cosine[...], sine[...] = angles(places[...])
    for load in loads[1:]:
        load.wait()
    window = 2
    units = [(PAIR, i) for i in range(own_heads)] + [(QUERY, i) for i in range(own_heads)]

    def go_on(n, apart):
        z_copy(*units[n], apart).wait_send()
        if n + window < len(units):
            z_copy(*units[n + window], apart).start()

    for i in range(own_heads):
        for apart in order:
            prepare_pair(at_layer(apart) * own_heads + i, stage, i, apart)
            if i == 0 and apart == order[0]:
                pl.semaphore_wait(barrier, len(peers))
            if i < window:
                z_copy(PAIR, i, apart).start()
        prepare_pair(layer * own_heads + i, own, i, layer)
        x_copy(i, layer).start()
    for i in range(own_heads):
        for apart in order:
            prepare_queries(at_layer(apart) * own_heads + i, stage, i, apart)
        prepare_queries(layer * own_heads + i, own, i, layer)

    def relay(i):
        for source in range(layers):
            x_copy(i, source).wait_recv()
        core_copy(i, 1).start()

    for i in range(own_heads):
        for apart in order:
            z_arrival(PAIR, i, apart).wait_recv()
            x_copy(i, at_layer(layers - apart)).start()
            go_on(i, apart)
        core_copy(i, 0).start()
        if i:
            relay(i - 1)
    relay(own_heads - 1)

    factor = math.log2(math.e) / math.sqrt(HEAD_DIM)

    def step(i):
        for apart in order:
            z_arrival(QUERY, i, apart).wait_recv()
            go_on(own_heads + i, apart)
        queries = own[i, 0].reshape(rows, HEAD_DIM)

        def block(state, keys, values):
            scores = lax.dot_general(
                queries, keys.reshape(rows, HEAD_DIM), (((1,), (1,)), ((), ())),
                preferred_element_type=jnp.float32,
            ) * factor
            top = jnp.max(scores, axis=-1, keepdims=True)
            if state is not None:
                top = jnp.maximum(top, state[0])
            expo = jnp.exp2(scores - top)
            total = jnp.sum(expo, axis=-1, keepdims=True)
            mixed = jnp.dot(
                expo.astype(jnp.bfloat16), values.reshape(rows, HEAD_DIM),
                preferred_element_type=jnp.float32,
            )
            if state is not None:
                fade = jnp.exp2(state[0] - top)
                total = total + state[1] * fade
                mixed = mixed + state[2] * fade
            return top, total, mixed

        state = block(None, own[i, 1], own[i, 2])
        state = block(state, from_x[i, 0], from_x[i, 1])
        core_copy(i, 0).wait_recv()
        state = block(state, from_core[i, 0, 0], from_core[i, 0, 1])
        core_copy(i, 1).wait_recv()
        _, total, mixed = block(state, from_core[i, 1, 0], from_core[i, 1, 1])
        out_stage[i] = (mixed / total).astype(jnp.bfloat16).reshape(layers, tokens, HEAD_DIM)
        for apart in order:
            out_copy(i, apart).start()
        out_all[layer * own_heads + i] = out_stage[i, layer]

    for i in range(own_heads):
        step(i)

    for i in range(own_heads):
        for apart in order:
            out_arrival(i, apart).wait_recv()
    for head in range(layers * own_heads):
        columns = slice(head * HEAD_DIM, (head + 1) * HEAD_DIM)
        txt_out[:, columns] = out_all[head, :texts]
        img_out[:, columns] = out_all[head, texts:]

    for i in range(own_heads):
        for apart in order:
            out_copy(i, apart).wait_send()
        for source in range(layers):
            x_copy(i, source).wait_send()
        core_copy(i, 0).wait_send()
        core_copy(i, 1).wait_send()


def per_device_fused(layers, txt_q, txt_k, txt_v, img_q, img_k, img_v, q_gain, k_gain, places):
    own_heads = HEADS // layers
    tokens = txt_q.shape[0] + img_q.shape[0]
    bf16, dma = jnp.bfloat16, pltpu.SemaphoreType.DMA
    block = (tokens, HEAD_DIM)
    hold = functools.partial(pltpu.with_memory_space_constraint, memory_space=pltpu.HBM)
    txt_q, txt_k, txt_v, img_q, img_k, img_v = map(hold, (txt_q, txt_k, txt_v, img_q, img_k, img_v))
    q_gain, k_gain, places = (hold(x.reshape(1, -1)) for x in (q_gain, k_gain, places))
    return pl.pallas_call(
        functools.partial(attention_kernel, layers, own_heads),
        out_shape=(
            jax.ShapeDtypeStruct(txt_q.shape, bf16),
            jax.ShapeDtypeStruct(img_q.shape, bf16),
        ),
        in_specs=[pl.BlockSpec(memory_space=pltpu.HBM)] * 9,
        out_specs=(pl.BlockSpec(memory_space=pltpu.VMEM),) * 2,
        scratch_shapes=[
            *[pltpu.VMEM(x.shape, bf16) for x in (txt_q, txt_k, txt_v, img_q, img_k, img_v)],
            pltpu.VMEM((1, HEAD_DIM), jnp.float32),
            pltpu.VMEM((1, HEAD_DIM), jnp.float32),
            pltpu.VMEM(places.shape, jnp.int32),
            pltpu.VMEM((img_q.shape[0], HEAD_DIM), jnp.float32),
            pltpu.VMEM((img_q.shape[0], HEAD_DIM), jnp.float32),
            dma((9,)),
            pltpu.VMEM((own_heads, 3, layers, *block), bf16),
            pltpu.VMEM((own_heads, 3, layers, *block), bf16),
            pltpu.VMEM((own_heads, 2, layers, *block), bf16),
            pltpu.VMEM((own_heads, 2, 2, layers, *block), bf16),
            pltpu.VMEM((own_heads, layers, *block), bf16),
            pltpu.VMEM((HEADS, *block), bf16),
            dma((own_heads, layers)), dma((own_heads, layers)),
            dma((own_heads, layers)), dma((own_heads, layers)),
            dma((own_heads, layers)), dma((own_heads, layers)),
            dma((own_heads, 2)), dma((own_heads, 2)),
            dma((own_heads, layers)), dma((HEADS,)),
        ],
        compiler_params=pltpu.CompilerParams(
            collective_id=0, has_side_effects=True, vmem_limit_bytes=40 * 1024 * 1024
        ),
    )(
        txt_q, txt_k, txt_v, img_q, img_k, img_v,
        q_gain, k_gain, places,
    )


def per_device_any(txt_q, txt_k, txt_v, img_q, img_k, img_v, q_gain, k_gain, places):
    layers, left_over = divmod(lax.axis_size("blk"), COLUMN)
    whole_tiles = txt_q.shape[0] % 16 == 0 and img_q.shape[0] % 16 == 0
    fits = left_over == 0 and layers > 1 and HEADS % max(layers, 1) == 0 and whole_tiles
    part = functools.partial(per_device_fused, layers) if fits else per_device
    return part(txt_q, txt_k, txt_v, img_q, img_k, img_v, q_gain, k_gain, places)


def solution(mesh):
    placed = (
        P(("groups", "blk"), None),
        P(("groups", "blk"), None),
        P(("groups", "blk"), None),
        P(("groups", "blk"), None),
        P(("groups", "blk"), None),
        P(("groups", "blk"), None),
        P(),
        P(),
        P(("groups", "blk")),
    )
    return jax.shard_map(
        per_device_any,
        mesh=mesh,
        in_specs=placed,
        out_specs=(P(("groups", "blk"), None), P(("groups", "blk"), None)),
        check_vma=False,
    )
```
